32 devices in a mesh: ens: 2 (over x), lon: 16 (over z, y, core).
Axes of the slice: x: 2, y: 2, z: 4, core: 2. Of those that a mesh axis runs over, the one named last changes fastest.
Arguments:
- state_in: bfloat16 [32, 128, 512], P('ens', 'lon'), parts along dimension 0, may hold values from -6 to 6
- ocean_mask: int32 [16, 128], P(None, 'lon'), may hold values 0 or 1
- fold_partner: int32 [128], replicated, may hold values from 0 to 127, as said below
- depth_kernel: float32 [49, 512], replicated, may hold values from -0.875 to 0.875
- norm_gain: float32 [512], replicated, may hold values from 0.1 to 1.9
- norm_bias: float32 [512], replicated, may hold values from -3 to 3
- w_up: bfloat16 [512, 2048], replicated, may hold values from -0.25 to 0.25
- w_down: bfloat16 [2048, 512], replicated, may hold values from -0.125 to 0.125
- cotangent: bfloat16 [32, 128, 512], P('ens', 'lon'), parts along dimension 0, may hold values from -8 to 8
Outputs:
- out_state: bfloat16 [32, 128, 512], P('ens', 'lon'), parts along dimension 0
- grad_state: bfloat16 [32, 128, 512], P('ens', 'lon'), parts along dimension 0
- grad_up: float32 [1024, 2048], P(('ens', 'lon')), parts along dimension 0
- grad_down: float32 [4096, 512], P(('ens', 'lon')), parts along dimension 0
- grad_kernel: float32 [98, 512], P('ens'), parts along dimension 0
- grad_gain: float32 [1024], P('ens'), parts along dimension 0
- grad_bias: float32 [1024], P('ens'), parts along dimension 0
The draws below stay inside these ranges and needn't reach their ends.
There are 2 independent parts, one for each index of `ens`. The reference program is written for one: setup_inputs(seed, part) draws one part's arguments, and reference() takes and returns one part's arrays. A program takes and returns all parts, laid end to end along the dimension named above; an argument that names none is the same for every part. Nothing has to cross between parts.
Inputs may be any that keep to these rules, and one draw needn't show every extreme that they name: fold_partner[i] == (P - i) mod 128 for every column i, with one whole number P of 0 to 127 in each draw.
All inputs are finite; a program needn't handle non-finite values. No bound on the sum of `ocean_mask` on one device may be relied on, other than what follows from the above.
Results may differ from the reference program's by a relative error of at most 0.0055.
Values may be sent and summed in bfloat16 or wider, within the bound.
A program may use at most 64 MiB of HBM per device.

```python
import math
import jax
import jax.numpy as jnp
from jax import lax

C = 512
HID = 2048
LAT = 16
LON = 128


def draw_fold_partner(key, part):
    key = jax.random.fold_in(key, 5)
    pivot_col = jax.random.randint(key, (), 0, LON)
    return ((pivot_col - jnp.arange(LON)) % LON).astype(jnp.int32)


def draw_cotangent(key, part):
    key = jax.random.fold_in(key, 11)
    key_base, key_rough = jax.random.split(key, 2)
    rising = 3.0 ** (jnp.arange(LON, dtype=jnp.float32) / LON)
    rough_scale = jnp.exp(jax.random.uniform(key_rough, (LAT, LON), jnp.float32, 0.0, 1.2))
    cell_scale = (rough_scale * rising[None, :])[:, :, None]
    values = 0.6 * jax.random.normal(key_base, (LAT, LON, C), jnp.float32) * cell_scale
    return jnp.clip(values, -8.0, 8.0).astype(jnp.bfloat16)


def plant(values, stream_key, least, top_value):
    longest = values.shape.index(max(values.shape))
    spots = []
    for shift in (0, 1):
        where = [jax.random.randint(jax.random.fold_in(stream_key, axis), (), 0, length) for axis, length in enumerate(values.shape)]
        where[longest] = (where[longest] + shift) % values.shape[longest]
        spots.append(tuple(where))
    return values.at[spots[0]].set(least).at[spots[1]].set(top_value)


def steps_of(key, dims, cuts, least, largest):
    loudness = 1.0
    for dim, parts in cuts:
        heights = jax.random.uniform(jax.random.fold_in(jax.random.fold_in(key, 6), dim), (parts,), jnp.float32, least / len(cuts), largest / len(cuts))
        loudness = loudness * jnp.repeat(jnp.exp(heights), dims[dim] // parts).reshape((-1,) + (1,) * (len(dims) - 1 - dim))
    return loudness


def bell_draw(own_key, extent, width, reach, cuts=(), kind=jnp.bfloat16):
    gain = steps_of(own_key, extent, cuts, -0.22, 0.18) if cuts else 1.0
    values = jax.random.normal(own_key, extent, jnp.float32) * width * gain
    return jnp.minimum(jnp.maximum(values, -reach), reach).astype(kind)


def setup_inputs(seed: int = 0, part: int = 0) -> dict:
    seeds = jax.random.split(jax.random.key(seed), 10)
    own_keys = jax.random.split(jax.random.fold_in(seeds[9], part), 10)
    state_in = bell_draw(own_keys[0], (LAT, LON, C), 1.0, 6.0, ((1, 16),))
    ocean_mask = plant((jax.random.randint(seeds[1], (LAT, LON), 0, 4) < 3).astype(jnp.int32), jax.random.fold_in(seeds[1], 1), 0, 1)
    fold_partner = draw_fold_partner(jax.random.fold_in(seeds[9], 71), part)
    depth_kernel = bell_draw(seeds[3], (49, C), 49 ** -0.5, 0.875, (), jnp.float32)
    norm_gain = jnp.clip(1.0 + 0.18 * jax.random.normal(seeds[4], (C,), jnp.float32), 0.1, 1.9)
    norm_bias = bell_draw(seeds[5], (C,), 0.5, 3.0, (), jnp.float32)
    w_up = bell_draw(seeds[6], (C, HID), C ** -0.5, 0.25)
    w_down = bell_draw(seeds[7], (HID, C), HID ** -0.5, 0.125)
    cotangent = draw_cotangent(jax.random.fold_in(jax.random.fold_in(seeds[9], part), 71), part)
    return {"state_in": state_in, "ocean_mask": ocean_mask, "fold_partner": fold_partner, "depth_kernel": depth_kernel, "norm_gain": norm_gain, "norm_bias": norm_bias, "w_up": w_up, "w_down": w_down, "cotangent": cotangent}


EPS = 1e-06

def gelu_value(values):
    return jax.nn.gelu(values, approximate=True)

def gelu_back(values, upstream):
    return jax.vjp(gelu_value, values)[1](upstream)[0]

def depth_conv(extended, depth_kernel):
    channels = extended.shape[2]
    result = lax.conv_general_dilated(extended[None], depth_kernel.reshape(7, 7, 1, channels), (1, 1), 'VALID', dimension_numbers=('NHWC', 'HWIO', 'NHWC'), feature_group_count=channels, precision=lax.Precision.HIGHEST)
    return result[0]

def reference(state_in, ocean_mask, fold_partner, depth_kernel, norm_gain, norm_bias, w_up, w_down, cotangent):
    grad_scale = 1.0 / math.sqrt(LAT * LON)
    mask_float = ocean_mask.astype(jnp.float32)
    masked = state_in * ocean_mask[:, :, None].astype(jnp.bfloat16)
    zonal_ext = jnp.concatenate([masked[:, LON - 3:], masked, masked[:, :3]], axis=1)
    ext_cols = ((jnp.arange(LON + 6) - 3) % LON).astype(jnp.int32)
    north_rows = jnp.take(masked[LAT - 3:], jnp.take(fold_partner, ext_cols), axis=1)[::-1]
    south_pad = jnp.zeros((3, LON + 6, C), jnp.bfloat16)
    extended = jnp.concatenate([south_pad, zonal_ext, north_rows], axis=0).astype(jnp.float32)
    conv_out, conv_back = jax.vjp(depth_conv, extended, depth_kernel)

    def row_step(sums_in, inputs):
        grad_up, grad_down, gain_sum, bias_sum = sums_in
        conv_row, state_row, mask_row, cot_row = inputs
        centred = conv_row - lax.optimization_barrier(jnp.mean(conv_row, axis=1, keepdims=True))
        inv_std = 1.0 / jnp.sqrt(lax.optimization_barrier(jnp.mean(centred * centred, axis=1, keepdims=True)) + EPS)
        normed = centred * inv_std
        norm_out = (normed * norm_gain + norm_bias).astype(jnp.bfloat16)
        pre_act = jnp.dot(norm_out, w_up, preferred_element_type=jnp.float32)
        hidden_u = gelu_value(pre_act).astype(jnp.bfloat16)
        branch = jnp.dot(hidden_u, w_down, preferred_element_type=jnp.float32)
        out_row = (state_row.astype(jnp.float32) + mask_row[:, None] * branch).astype(jnp.bfloat16)
        upstream = cot_row * mask_row[:, None].astype(jnp.bfloat16)
        grad_down = grad_down + lax.dot_general(hidden_u, upstream, (((0,), (0,)), ((), ())), preferred_element_type=jnp.float32)
        grad_hidden = lax.dot_general(upstream, w_down, (((1,), (1,)), ((), ())), preferred_element_type=jnp.float32)
        grad_pre = gelu_back(pre_act, grad_hidden).astype(jnp.bfloat16)
        grad_up = grad_up + lax.dot_general(norm_out, grad_pre, (((0,), (0,)), ((), ())), preferred_element_type=jnp.float32)
        grad_norm = lax.dot_general(grad_pre, w_up, (((1,), (1,)), ((), ())), preferred_element_type=jnp.float32)
        gain_sum = gain_sum + lax.optimization_barrier(jnp.sum(grad_norm * normed, axis=0))
        bias_sum = bias_sum + lax.optimization_barrier(jnp.sum(grad_norm, axis=0))
        scaled = grad_norm * norm_gain
        grad_conv = (scaled - lax.optimization_barrier(jnp.mean(scaled, axis=1, keepdims=True)) - normed * lax.optimization_barrier(jnp.mean(scaled * normed, axis=1, keepdims=True))) * inv_std
        return ((grad_up, grad_down, gain_sum, bias_sum), (out_row, grad_conv))
    start_sums = (jnp.zeros((C, HID), jnp.float32), jnp.zeros((HID, C), jnp.float32), jnp.zeros((C,), jnp.float32), jnp.zeros((C,), jnp.float32))
    final_sums, per_row = lax.scan(row_step, start_sums, (conv_out, state_in, mask_float, cotangent))
    grad_up, grad_down, gain_sum, bias_sum = final_sums
    out_state, grad_conv = per_row
    grad_ext, kernel_sum = conv_back(grad_conv)
    middle = grad_ext[3:]
    inner_grad = middle[:, 3:LON + 3]
    inner_grad = inner_grad.at[:, :3].add(middle[:, LON + 3:])
    inner_grad = inner_grad.at[:, LON - 3:].add(middle[:, :3])
    folded = jnp.take(inner_grad[LAT:], fold_partner, axis=1)[::-1]
    grad_masked = inner_grad[:LAT].at[LAT - 3:].add(folded)
    grad_state = (cotangent.astype(jnp.float32) + mask_float[:, :, None] * grad_masked).astype(jnp.bfloat16)
    return (out_state, grad_state, grad_up * grad_scale, grad_down * grad_scale, kernel_sum * grad_scale, gain_sum * grad_scale, bias_sum * grad_scale)
```

```python
import functools
import math

import jax
import jax.numpy as jnp
import numpy as np
from jax import lax
from jax.experimental import pallas as pl
from jax.experimental.pallas import tpu as pltpu
from jax.sharding import PartitionSpec as P

EPS = 1e-06
TILE = 512
BF = jnp.bfloat16
F32 = jnp.float32
GELU_A = math.sqrt(2.0 / math.pi)
GELU_B = 0.044715


def shift_matrices(lat, cols):
    own0, right0 = 3 * lat, 3 * lat + lat * cols
    depth = -(-(right0 + 3 * lat) // 128) * 128
    shifts = np.zeros((7, lat, cols, depth), np.float32)
    for b in range(7):
        for i in range(cols):
            e = b + i
            for r in range(lat):
                if e < 3:
                    src = r * 3 + e
                elif e < cols + 3:
                    src = own0 + r * cols + e - 3
                else:
                    src = right0 + r * 3 + e - cols - 3
                shifts[b, r, i, src] = 1.0
    packs = np.zeros((2, lat, 3, lat * cols), np.float32)
    for r in range(lat):
        for k in range(3):
            packs[0, r, k, r * cols + k] = 1.0
            packs[1, r, k, r * cols + cols - 3 + k] = 1.0
    return shifts.reshape(7 * lat * cols, depth), packs.reshape(6 * lat, lat * cols)


def place(chunk, order):
    pos = 0
    for bit in order:
        pos = pos * 2 + (chunk // 2**bit) % 2
    return pos


def dot(a, b, dims=((1,), (0,))):
    return lax.dot_general(a, b, (dims, ((), ())), preferred_element_type=F32)


def kernel(
    n, lat, cols,
    fold_ref, state_ref, mask_ref, dk_ref, gain_ref, bias_ref, cot_ref, shift_ref, pack_ref, wup_hbm, wdn_hbm,
    out_ref, gstate_ref, gup_ref, gdn_ref, gk_ref, ggain_ref, gbias_ref,
    wup, wdn, ext, ext_g, pk, pk_g, top, top_g, sh, sh_g, sh_f, norm_s, nout_s, inv_s, ups, br, gn, gc,
    acc_d, acc_u, snd_d, snd_u, rcv_d, rcv_u, smb, smr,
    w_sem, h_send, h_recv, t_send, t_recv, d_send, d_recv, u_send, u_recv, s_send, s_recv,
):
    chans = state_ref.shape[1]
    hid = wup.shape[1]
    cells = lat * cols
    total = n * cols
    logn = n.bit_length() - 1
    scale = 1.0 / math.sqrt(lat * total)
    me = lax.axis_index("lon")
    order_d = list(range(logn))
    order_u = [0, 2, 1] + list(range(3, logn))
    right, left = (me + 1) % n, (me + n - 1) % n
    half_c = chans // 2

    w_copies = [
        pltpu.make_async_copy(wup_hbm, wup, w_sem.at[0]),
        pltpu.make_async_copy(wdn_hbm, wdn, w_sem.at[1]),
    ]
    for c in w_copies:
        c.start()

    barrier = pltpu.get_barrier_semaphore()

    @pl.loop(1, n)
    def _(k):
        pl.semaphore_signal(barrier, inc=1, device_id={"lon": (me + k) % n}, device_id_type=pl.DeviceIdType.MESH)

    mask = mask_ref[...]
    mask_bf = mask.astype(BF)

    def remote(src, dst, ss, rs, dev):
        return pltpu.make_async_remote_copy(
            src_ref=src, dst_ref=dst, send_sem=ss, recv_sem=rs,
            device_id={"lon": dev}, device_id_type=pl.DeviceIdType.MESH,
        )

    own0, right0, edge = 3 * lat, 3 * lat + cells, 3 * lat

    def halo_copies(e_ref, p_ref, w):
        return [
            remote(p_ref.at[pl.ds(edge, edge)], e_ref.at[pl.ds(0, edge)], h_send.at[2 * w], h_recv.at[2 * w], right),
            remote(p_ref.at[pl.ds(0, edge)], e_ref.at[pl.ds(right0, edge)], h_send.at[2 * w + 1], h_recv.at[2 * w + 1], left),
        ]

    def top_copy(t_ref, w, k):
        return remote(t_ref.at[me], t_ref.at[me], t_send.at[w * n + k], t_recv.at[w * n + k], (me + k) % n)

    def prepare(e_ref, p_ref, t_ref, values_bf):
        e_ref[pl.ds(own0, cells), :] = values_bf
        e_ref[pl.ds(right0 + edge, e_ref.shape[0] - right0 - edge), :] = jnp.zeros(
            (e_ref.shape[0] - right0 - edge, chans), BF)
        p_ref[...] = dot(pack_ref[...], values_bf).astype(BF)
        for k in range(3):
            row = values_bf[(lat - 3 + k) * cols:(lat - 2 + k) * cols].astype(F32)
            t_ref[me, pl.ds(k * 2 * cols, 2 * cols), :] = jnp.concatenate(
                [row[:, :half_c], row[:, half_c:]], axis=0).astype(BF)

    def send_all(e_ref, p_ref, t_ref, w):
        for c in halo_copies(e_ref, p_ref, w):
            c.start()

        @pl.loop(1, n)
        def _(k):
            top_copy(t_ref, w, k).start()

    def wait_halo(e_ref, p_ref, w):
        for c in halo_copies(e_ref, p_ref, w):
            c.wait_recv()

    def wait_top(t_ref, w):
        @pl.loop(1, n)
        def _(k):
            top_copy(t_ref, w, k).wait_recv()

    def put_shifts(e_ref, s_ref):
        s_ref[:, pl.ds(0, 3)] = jnp.zeros((7, 3, cols, chans), F32)
        for b in range(7):
            part = dot(shift_ref[pl.ds(b * cells, cells), :], e_ref[...])
            s_ref[b, pl.ds(3, lat)] = part.reshape(lat, cols, chans)

    def put_fold(t_ref, sel, store):
        for k in range(3):
            rows = t_ref[:, pl.ds(k * 2 * cols, 2 * cols), :].reshape(n * 2 * cols, half_c)
            got = dot(sel, rows).reshape(2, 7, cols, half_c)
            for h in range(2):
                for b in range(7):
                    store(k, b, pl.ds(h * half_c, half_c), got[h, b])

    def lanes(ct):
        return pl.ds(pl.multiple_of(ct * 128, 128), 128)

    state = state_ref[...]
    prepare(ext, pk, top, state * mask_bf)
    pl.semaphore_wait(barrier, n - 1)
    send_all(ext, pk, top, 0)

    m_id = lax.broadcasted_iota(jnp.int32, (14 * cols, n * 2 * cols), 0)
    q_id = lax.broadcasted_iota(jnp.int32, (14 * cols, n * 2 * cols), 1)
    half_m = jnp.where(m_id >= 7 * cols, 1, 0)
    m_in = m_id - half_m * (7 * cols)
    want = fold_ref[0] - me * cols + 3 - (m_in // cols + m_in % cols)
    want = jnp.where(want < 0, want + total, want)
    want = jnp.where(want < 0, want + total, want)
    want = jnp.where(want >= total, want - total, want)
    have = (q_id // (2 * cols)) * cols + q_id % cols
    half_q = (q_id // cols) % 2
    sel = jnp.where((have == want) & (half_q == half_m), 1.0, 0.0).astype(BF)

    cot = cot_ref[...]
    upstream = cot * mask_bf
    ups[...] = upstream

    wait_halo(ext, pk, 0)
    put_shifts(ext, sh)
    wait_top(top, 0)

    def store_north(k, b, ls, val):
        sh[b, lat + 5 - k, :, ls] = val

    put_fold(top, sel, store_north)

    @pl.loop(0, chans // 128)
    def _(ct):
        ls = lanes(ct)
        acc = jnp.zeros((lat, cols, 128), F32)
        for b in range(7):
            window = sh[b, :, :, ls]
            for a in range(7):
                tap = dk_ref[pl.ds(7 * a + b, 1), ls].reshape(1, 1, 128)
                acc = acc + tap * window[a:a + lat]
        norm_s[:, ls] = acc.reshape(cells, 128)

    conv = norm_s[...]
    centred = conv - jnp.mean(conv, axis=1, keepdims=True)
    inv = 1.0 / jnp.sqrt(jnp.mean(centred * centred, axis=1, keepdims=True) + EPS)
    inv_s[...] = inv
    normed = centred * inv
    norm_s[...] = normed
    nout_s[...] = (normed * gain_ref[...] + bias_ref[...]).astype(BF)
    for c in w_copies:
        c.wait()
    br[...] = jnp.zeros_like(br)
    gn[...] = jnp.zeros_like(gn)
    rows_d, rows_u = hid // n, chans // n
    per_tile = TILE // rows_d

    @pl.loop(0, hid // TILE)
    def _(t):
        hs = pl.ds(pl.multiple_of(t * TILE, TILE), TILE)
        nout = nout_s[...]
        up = ups[...]
        w1 = wup[:, hs]
        w2 = wdn[hs, :]
        v = dot(nout, w1)
        v2 = v * v
        th = jnp.tanh(GELU_A * (v + GELU_B * (v2 * v)))
        u = (0.5 * v * (1.0 + th)).astype(BF)
        br[...] += dot(u, w2)
        gd = dot(u, up, ((0,), (0,)))
        for cc in range(per_tile):
            pos = place(t * per_tile + cc, order_d)
            acc_d[pl.ds(pl.multiple_of(pos * rows_d, 8), rows_d), :] = gd[cc * rows_d:(cc + 1) * rows_d]
        gh = dot(up, w2, ((1,), (1,)))
        slope = 0.5 * (1.0 + th) + (0.5 * GELU_A) * v * (1.0 - th * th) * (1.0 + (3.0 * GELU_B) * v2)
        gp = (gh * slope).astype(BF)
        gn[...] += dot(gp, w1, ((1,), (1,)))
        gu = dot(nout, gp, ((0,), (0,)))
        for c in range(n):
            base = place(c, order_u) * (hid * chans // n // TILE)
            acc_u[pl.ds(pl.multiple_of(base + t * rows_u, 8), rows_u), :] = gu[c * rows_u:(c + 1) * rows_u]

    def bit_of(bit):
        return (me // 2**bit) % 2

    def partner(bit):
        return me + (1 - 2 * bit_of(bit)) * 2**bit

    size = acc_d.shape[0]

    def rs_base(order, s):
        base = 0
        for k in range(s):
            base = base + bit_of(order[k]) * (size >> (k + 1))
        return base

    def rs_copy(snd, rcv, ss, rs, order, s):
        off, half = size - (size >> s), size >> (s + 1)
        return remote(snd.at[pl.ds(off, half)], rcv.at[pl.ds(off, half)], ss.at[s], rs.at[s], partner(order[s]))

    def rs_send(acc, snd, rcv, ss, rs, order, s):
        off, half = size - (size >> s), size >> (s + 1)
        base = rs_base(order, s) + (1 - bit_of(order[s])) * half
        blk = min(64, half)

        @pl.loop(0, half // blk)
        def _(i):
            snd[pl.ds(pl.multiple_of(off + i * blk, 16), blk), :] = acc[
                pl.ds(pl.multiple_of(base + i * blk, 16), blk), :].astype(BF)

        rs_copy(snd, rcv, ss, rs, order, s).start()

    def rs_recv(acc, snd, rcv, ss, rs, order, s):
        off, half = size - (size >> s), size >> (s + 1)
        base = rs_base(order, s + 1)
        blk = min(64, half)
        rs_copy(snd, rcv, ss, rs, order, s).wait_recv()

        @pl.loop(0, half // blk)
        def _(i):
            at = pl.ds(pl.multiple_of(base + i * blk, 16), blk)
            acc[at, :] += rcv[pl.ds(pl.multiple_of(off + i * blk, 16), blk), :].astype(F32)

    down = (acc_d, snd_d, rcv_d, d_send, d_recv, order_d)
    upw = (acc_u, snd_u, rcv_u, u_send, u_recv, order_u)
    rs_send(*down, 0)
    rs_send(*upw, 0)

    gnorm = gn[...]
    normed = norm_s[...]
    gain_row = jnp.sum(gnorm * normed, axis=0, keepdims=True)
    bias_row = jnp.sum(gnorm, axis=0, keepdims=True)
    scaled = gnorm * gain_ref[...]
    grad_conv = (
        scaled
        - jnp.mean(scaled, axis=1, keepdims=True)
        - normed * jnp.mean(scaled * normed, axis=1, keepdims=True)
    ) * inv_s[...]
    gc[...] = grad_conv
    prepare(ext_g, pk_g, top_g, grad_conv.astype(BF))
    send_all(ext_g, pk_g, top_g, 1)
    taps = dk_ref.shape[0]
    smb[0, pl.ds(48, 8), :] = jnp.zeros((8, chans), F32)
    smb[0, pl.ds(taps, 1), :] = gain_row
    smb[0, pl.ds(taps + 1, 1), :] = bias_row

    out_ref[...] = (state_ref[...].astype(F32) + mask * br[...]).astype(BF)

    rs_recv(*down, 0)
    rs_send(*down, 1)
    rs_recv(*upw, 0)
    rs_send(*upw, 1)

    @pl.loop(0, chans // 128)
    def _(ct):
        ls = lanes(ct)
        g = gc[:, ls].reshape(lat, cols, 128)
        for b in range(7):
            window = sh[b, :, :, ls]
            for a in range(7):
                part = jnp.sum(g * window[a:a + lat], axis=0)
                smb[0, pl.ds(7 * a + b, 1), ls] = jnp.sum(part, axis=0, keepdims=True)

    def sm_copy(s):
        return remote(smb.at[s], smr.at[s], s_send.at[s], s_recv.at[s], partner(s))

    def sm_step(s):
        sm_copy(s).wait_recv()
        smb[s + 1] = smb[s] + smr[s]
        if s + 1 < logn:
            sm_copy(s + 1).start()

    sm_copy(0).start()

    wait_halo(ext_g, pk_g, 1)
    put_shifts(ext_g, sh_g)
    sh_g[:, pl.ds(lat + 3, 3)] = jnp.zeros((7, 3, cols, chans), F32)
    sm_step(0)
    wait_top(top_g, 1)

    def store_facing(k, b, ls, val):
        sh_f[b, k, :, ls] = val

    put_fold(top_g, sel, store_facing)

    @pl.loop(0, chans // 128)
    def _(ct):
        ls = lanes(ct)
        acc = jnp.zeros((lat, cols, 128), F32)
        fold = [jnp.zeros((cols, 128), F32) for _ in range(3)]
        for b in range(7):
            window = sh_g[b, :, :, ls]
            for a in range(7):
                tap = dk_ref[pl.ds(48 - (7 * a + b), 1), ls].reshape(1, 1, 128)
                acc = acc + tap * window[a:a + lat]
            for r in range(3):
                for j in range(3):
                    a = 8 - r - j
                    if a <= 6:
                        tap = dk_ref[pl.ds(7 * a + b, 1), ls]
                        fold[r] = fold[r] + tap * sh_f[b, j, :, ls]
        acc = acc.reshape(cells, 128)
        gc[:, ls] = acc
        for r in range(3):
            gc[pl.ds((lat - 3 + r) * cols, cols), ls] += fold[r]

    gstate_ref[...] = (cot_ref[...].astype(F32) + mask * gc[...]).astype(BF)

    for s in range(1, logn):
        rs_recv(*down, s)
        if s + 1 < logn:
            rs_send(*down, s + 1)
        rs_recv(*upw, s)
        if s + 1 < logn:
            rs_send(*upw, s + 1)
        sm_step(s)

    base_d = pl.multiple_of(rs_base(order_d, logn), 8)
    base_u = rs_base(order_u, logn)
    gdn_ref[...] = acc_d[pl.ds(base_d, rows_d), :] * scale
    for t in range(hid // TILE):
        gup_ref[:, pl.ds(t * TILE, TILE)] = acc_u[pl.ds(pl.multiple_of(base_u + t * rows_u, 8), rows_u), :] * scale
    gk_ref[...] = smb[logn, pl.ds(0, taps), :] * scale
    ggain_ref[...] = smb[logn, pl.ds(taps, 1), :] * scale
    gbias_ref[...] = smb[logn, pl.ds(taps + 1, 1), :] * scale

    for e_ref, p_ref, t_ref, w in ((ext, pk, top, 0), (ext_g, pk_g, top_g, 1)):
        for c in halo_copies(e_ref, p_ref, w):
            c.wait_send()

        @pl.loop(1, n)
        def _(k):
            top_copy(t_ref, w, k).wait_send()

    for s in range(logn):
        rs_copy(*down[1:], s).wait_send()
        rs_copy(*upw[1:], s).wait_send()
        sm_copy(s).wait_send()


def on_device(
    state_in, ocean_mask, fold_partner, depth_kernel, norm_gain, norm_bias, w_up, w_down, cotangent
):
    lat, cols, chans = state_in.shape
    hid = w_up.shape[1]
    n = lax.axis_size("lon")
    logn = n.bit_length() - 1
    cells = lat * cols
    shifts, packs = shift_matrices(lat, cols)
    depth = shifts.shape[1]
    rows = hid * chans // TILE
    vm = pl.BlockSpec(memory_space=pltpu.VMEM)
    sem = pltpu.SemaphoreType.DMA
    outs = pl.pallas_call(
        functools.partial(kernel, n, lat, cols),
        out_shape=(
            jax.ShapeDtypeStruct((cells, chans), BF),
            jax.ShapeDtypeStruct((cells, chans), BF),
            jax.ShapeDtypeStruct((chans // n, hid), F32),
            jax.ShapeDtypeStruct((hid // n, chans), F32),
            jax.ShapeDtypeStruct(depth_kernel.shape, F32),
            jax.ShapeDtypeStruct((1, chans), F32),
            jax.ShapeDtypeStruct((1, chans), F32),
        ),
        in_specs=[pl.BlockSpec(memory_space=pltpu.SMEM)] + [vm] * 8 + [pl.BlockSpec(memory_space=pl.ANY)] * 2,
        out_specs=(vm,) * 7,
        scratch_shapes=[
            pltpu.VMEM((chans, hid), BF),
            pltpu.VMEM((hid, chans), BF),
            pltpu.VMEM((depth, chans), BF),
            pltpu.VMEM((depth, chans), BF),
            pltpu.VMEM((6 * lat, chans), BF),
            pltpu.VMEM((6 * lat, chans), BF),
            pltpu.VMEM((n, 6 * cols, chans // 2), BF),
            pltpu.VMEM((n, 6 * cols, chans // 2), BF),
            pltpu.VMEM((7, lat + 6, cols, chans), F32),
            pltpu.VMEM((7, lat + 6, cols, chans), F32),
            pltpu.VMEM((7, 3, cols, chans), F32),
            pltpu.VMEM((cells, chans), F32),
            pltpu.VMEM((cells, chans), BF),
            pltpu.VMEM((cells, 1), F32),
            pltpu.VMEM((cells, chans), BF),
            pltpu.VMEM((cells, chans), F32),
            pltpu.VMEM((cells, chans), F32),
            pltpu.VMEM((cells, chans), F32),
            pltpu.VMEM((rows, TILE), F32),
            pltpu.VMEM((rows, TILE), F32),
            pltpu.VMEM((rows, TILE), BF),
            pltpu.VMEM((rows, TILE), BF),
            pltpu.VMEM((rows, TILE), BF),
            pltpu.VMEM((rows, TILE), BF),
            pltpu.VMEM((logn + 1, 56, chans), F32),
            pltpu.VMEM((logn, 56, chans), F32),
            sem((2,)),
            sem((4,)),
            sem((4,)),
            sem((2 * n,)),
            sem((2 * n,)),
            sem((logn,)),
            sem((logn,)),
            sem((logn,)),
            sem((logn,)),
            sem((logn,)),
            sem((logn,)),
        ],
        compiler_params=pltpu.CompilerParams(
            collective_id=0, has_side_effects=True, vmem_limit_bytes=52 * 1024 * 1024
        ),
    )(
        fold_partner,
        state_in.reshape(cells, chans),
        ocean_mask.astype(F32).reshape(cells, 1),
        depth_kernel,
        norm_gain.reshape(1, chans),
        norm_bias.reshape(1, chans),
        cotangent.reshape(cells, chans),
        jnp.asarray(shifts, BF),
        jnp.asarray(packs, BF),
        w_up,
        w_down,
    )
    out, gstate, gup, gdn, gk, ggain, gbias = outs
    return (
        out.reshape(lat, cols, chans),
        gstate.reshape(lat, cols, chans),
        gup,
        gdn,
        gk,
        ggain.reshape(chans),
        gbias.reshape(chans),
    )


def solution(mesh):
    return jax.shard_map(
        on_device,
        mesh=mesh,
        in_specs=(
            P("ens", "lon", None),
            P(None, "lon"),
            P(),
            P(),
            P(),
            P(),
            P(),
            P(),
            P("ens", "lon", None),
        ),
        out_specs=(
            P("ens", "lon", None),
            P("ens", "lon", None),
            P(("ens", "lon"), None),
            P(("ens", "lon"), None),
            P("ens", None),
            P("ens"),
            P("ens"),
        ),
        check_vma=False,
    )
```

```python
import functools
import math

import jax
import jax.numpy as jnp
import numpy as np
from jax import lax
from jax.experimental import pallas as pl
from jax.experimental.pallas import tpu as pltpu
from jax.sharding import PartitionSpec as P

EPS = 1e-06
TILE = 512
LANES = 256
BF = jnp.bfloat16
F32 = jnp.float32
GELU_A = math.sqrt(2.0 / math.pi)
GELU_B = 0.044715


def shift_matrices(lat, cols):
    own0, right0 = 3 * lat, 3 * lat + lat * cols
    depth = -(-(right0 + 3 * lat) // 128) * 128
    shifts = np.zeros((7, lat, cols, depth), np.float32)
    for b in range(7):
        for i in range(cols):
            e = b + i
            for r in range(lat):
                if e < 3:
                    src = r * 3 + e
                elif e < cols + 3:
                    src = own0 + r * cols + e - 3
                else:
                    src = right0 + r * 3 + e - cols - 3
                shifts[b, r, i, src] = 1.0
    packs = np.zeros((2, lat, 3, lat * cols), np.float32)
    for r in range(lat):
        for k in range(3):
            packs[0, r, k, r * cols + k] = 1.0
            packs[1, r, k, r * cols + cols - 3 + k] = 1.0
    return shifts.reshape(7 * lat * cols, depth), packs.reshape(6 * lat, lat * cols)


def place(chunk, order):
    pos = 0
    for bit in order:
        pos = pos * 2 + (chunk // 2**bit) % 2
    return pos


def dot(a, b, dims=((1,), (0,))):
    return lax.dot_general(a, b, (dims, ((), ())), preferred_element_type=F32)


def kernel(
    n, lat, cols,
    fold_ref, state_hbm, mask_hbm, pack_hbm, shift_hbm, dk_hbm, gain_hbm, bias_hbm, cot_hbm, wup_hbm, wdn_hbm,
    out_ref, gstate_ref, gup_ref, gdn_ref, gk_ref, ggain_ref, gbias_ref,
    state_ref, mask_ref, pack_ref, shift_ref, dk_ref, gain_ref, bias_ref, cot_ref, wup, wdn, ext, ext_g, pk, pk_g, top, top_g, sh, sh_g, sh_f, norm_s, nout_s, inv_s, ups, br, gn, gc,
    acc_d, acc_u, snd_d, snd_u, rcv_d, rcv_u, sm, sm_r, cur, cur_r, sums_s,
    w_sem, h_send, h_recv, t_send, t_recv, d_send, d_recv, u_send, u_recv, s_send, s_recv,
):
    chans = state_ref.shape[1]
    hid = wup.shape[1]
    cells = lat * cols
    total = n * cols
    logn = n.bit_length() - 1
    scale = 1.0 / math.sqrt(lat * total)
    me = lax.axis_index("lon")
    order_d = list(range(logn))
    order_u = [0, 2, 1] + list(range(3, logn))
    right, left = (me + 1) % n, (me + n - 1) % n
    half_c = chans // 2

    loads = [
        pltpu.make_async_copy(src, dst, w_sem.at[i])
        for i, (src, dst) in enumerate((
            (state_hbm, state_ref), (mask_hbm, mask_ref), (pack_hbm, pack_ref), (shift_hbm, shift_ref),
            (dk_hbm, dk_ref), (gain_hbm, gain_ref), (bias_hbm, bias_ref), (cot_hbm, cot_ref),
            (wup_hbm, wup), (wdn_hbm, wdn)))
    ]
    for c in loads:
        c.start()

    barrier = pltpu.get_barrier_semaphore()

    @pl.loop(1, n)
    def _(k):
        pl.semaphore_signal(barrier, inc=1, device_id={"lon": (me + k) % n}, device_id_type=pl.DeviceIdType.MESH)

    for c in loads[:3]:
        c.wait()
    mask = mask_ref[...]
    mask_bf = mask.astype(BF)

    def remote(src, dst, ss, rs, dev):
        return pltpu.make_async_remote_copy(
            src_ref=src, dst_ref=dst, send_sem=ss, recv_sem=rs,
            device_id={"lon": dev}, device_id_type=pl.DeviceIdType.MESH,
        )

    own0, right0, edge = 3 * lat, 3 * lat + cells, 3 * lat

    def halo_copies(e_ref, p_ref, w):
        return [
            remote(p_ref.at[pl.ds(edge, edge)], e_ref.at[pl.ds(0, edge)], h_send.at[2 * w], h_recv.at[2 * w], right),
            remote(p_ref.at[pl.ds(0, edge)], e_ref.at[pl.ds(right0, edge)], h_send.at[2 * w + 1], h_recv.at[2 * w + 1], left),
        ]

    mine, pairs = me % 2, n // 2

    def top_copy(t_ref, w, k):
        block = t_ref.at[mine, me // 2]
        at = w * (pairs + 1) + k
        return remote(block, block, t_send.at[at], t_recv.at[at], (me + 2 * k) % n)

    def pair_copy(t_ref, w):
        at = w * (pairs + 1) + pairs
        return remote(t_ref.at[mine], t_ref.at[mine], t_send.at[at], t_recv.at[at], me + 1 - 2 * mine)

    def prepare(e_ref, p_ref, t_ref, values_bf):
        e_ref[pl.ds(own0, cells), :] = values_bf
        e_ref[pl.ds(right0 + edge, e_ref.shape[0] - right0 - edge), :] = jnp.zeros(
            (e_ref.shape[0] - right0 - edge, chans), BF)
        p_ref[...] = dot(pack_ref[...], values_bf).astype(BF)
        for k in range(3):
            row = values_bf[(lat - 3 + k) * cols:(lat - 2 + k) * cols].astype(F32)
            t_ref[mine, me // 2, pl.ds(k * 2 * cols, 2 * cols), :] = jnp.concatenate(
                [row[:, :half_c], row[:, half_c:]], axis=0).astype(BF)

    def send_all(e_ref, p_ref, t_ref, w):
        for c in halo_copies(e_ref, p_ref, w):
            c.start()

        @pl.loop(1, pairs)
        def _(k):
            top_copy(t_ref, w, k).start()

    def wait_halo(e_ref, p_ref, w):
        for c in halo_copies(e_ref, p_ref, w):
            c.wait_recv()

    def pass_top(t_ref, w):
        @pl.loop(1, pairs)
        def _(k):
            top_copy(t_ref, w, k).wait_recv()

        pair_copy(t_ref, w).start()

    def wait_top(t_ref, w):
        pair_copy(t_ref, w).wait_recv()

    def put_shifts(e_ref, s_ref):
        s_ref[:, pl.ds(0, 3)] = jnp.zeros((7, 3, cols, chans), F32)
        for b in range(7):
            part = dot(shift_ref[pl.ds(b * cells, cells), :], e_ref[...])
            s_ref[b, pl.ds(3, lat)] = part.reshape(lat, cols, chans)

    def put_fold(t_ref, sel, store):
        for k in range(3):
            rows = t_ref[:, :, pl.ds(k * 2 * cols, 2 * cols), :].reshape(n * 2 * cols, half_c)
            got = dot(sel, rows).reshape(2, 7, cols, half_c)
            for h in range(2):
                for b in range(7):
                    store(k, b, pl.ds(h * half_c, half_c), got[h, b])

    def lanes(ct):
        return pl.ds(pl.multiple_of(ct * 128, 128), 128)

    state = state_ref[...]
    prepare(ext, pk, top, state * mask_bf)
    pl.semaphore_wait(barrier, n - 1)
    send_all(ext, pk, top, 0)

    m_id = lax.broadcasted_iota(jnp.int32, (14 * cols, n * 2 * cols), 0)
    q_id = lax.broadcasted_iota(jnp.int32, (14 * cols, n * 2 * cols), 1)
    half_m = jnp.where(m_id >= 7 * cols, 1, 0)
    m_in = m_id - half_m * (7 * cols)
    want = fold_ref[0] - me * cols + 3 - (m_in // cols + m_in % cols)
    want = jnp.where(want < 0, want + total, want)
    want = jnp.where(want < 0, want + total, want)
    want = jnp.where(want >= total, want - total, want)
    slot = q_id // (2 * cols)
    have = (2 * (slot % pairs) + slot // pairs) * cols + q_id % cols
    half_q = (q_id // cols) % 2
    sel = jnp.where((have == want) & (half_q == half_m), 1.0, 0.0).astype(BF)

    for c in loads[3:8]:
        c.wait()
    cot = cot_ref[...]
    upstream = cot * mask_bf
    ups[...] = upstream

    wait_halo(ext, pk, 0)
    put_shifts(ext, sh)
    pass_top(top, 0)
    wait_top(top, 0)

    def store_north(k, b, ls, val):
        sh[b, lat + 5 - k, :, ls] = val

    put_fold(top, sel, store_north)

    @pl.loop(0, chans // 128)
    def _(ct):
        ls = lanes(ct)
        acc = jnp.zeros((lat, cols, 128), F32)
        for b in range(7):
            window = sh[b, :, :, ls]
            for a in range(7):
                tap = dk_ref[pl.ds(7 * a + b, 1), ls].reshape(1, 1, 128)
                acc = acc + tap * window[a:a + lat]
        norm_s[:, ls] = acc.reshape(cells, 128)

    conv = norm_s[...]
    centred = conv - jnp.mean(conv, axis=1, keepdims=True)
    inv = 1.0 / jnp.sqrt(jnp.mean(centred * centred, axis=1, keepdims=True) + EPS)
    inv_s[...] = inv
    normed = centred * inv
    norm_s[...] = normed
    nout_s[...] = (normed * gain_ref[...] + bias_ref[...]).astype(BF)
    for c in loads[8:]:
        c.wait()
    br[...] = jnp.zeros_like(br)
    gn[...] = jnp.zeros_like(gn)
    rows_d, rows_u = hid // n, chans // n
    per_tile = TILE // rows_d

    @pl.loop(0, hid // TILE)
    def _(t):
        hs = pl.ds(pl.multiple_of(t * TILE, TILE), TILE)
        nout = nout_s[...]
        up = ups[...]
        w1 = wup[:, hs]
        w2 = wdn[hs, :]
        v = dot(nout, w1)
        v2 = v * v
        th = jnp.tanh(GELU_A * (v + GELU_B * (v2 * v)))
        u = (0.5 * v * (1.0 + th)).astype(BF)
        br[...] += dot(u, w2)
        gd = dot(u, up, ((0,), (0,)))
        for cc in range(per_tile):
            pos = place(t * per_tile + cc, order_d)
            acc_d[pl.ds(pl.multiple_of(pos * rows_d, 8), rows_d), :] = gd[cc * rows_d:(cc + 1) * rows_d]
        gh = dot(up, w2, ((1,), (1,)))
        slope = 0.5 * (1.0 + th) + (0.5 * GELU_A) * v * (1.0 - th * th) * (1.0 + (3.0 * GELU_B) * v2)
        gp = (gh * slope).astype(BF)
        gn[...] += dot(gp, w1, ((1,), (1,)))
        gu = dot(nout, gp, ((0,), (0,)))
        for c in range(n):
            base = place(c, order_u) * (hid * chans // n // TILE)
            acc_u[pl.ds(pl.multiple_of(base + t * rows_u, 8), rows_u), :] = gu[c * rows_u:(c + 1) * rows_u]

    def bit_of(bit):
        return (me // 2**bit) % 2

    def partner(bit):
        return me + (1 - 2 * bit_of(bit)) * 2**bit

    size = acc_d.shape[0]

    def rs_base(order, s):
        base = 0
        for k in range(s):
            base = base + bit_of(order[k]) * (size >> (k + 1))
        return base

    def rs_copy(part, h, s):
        acc, snd, rcv, ss, rs, order = part
        at = pl.ds(size - (size >> s), size >> (s + 1))
        sem = h * logn + s
        return remote(snd.at[h, at], rcv.at[h, at], ss.at[sem], rs.at[sem], partner(order[s]))

    def rs_send(part, h, s):
        acc, snd, rcv, ss, rs, order = part
        off, half = size - (size >> s), size >> (s + 1)
        base = rs_base(order, s) + (1 - bit_of(order[s])) * half
        blk = min(128, half)

        @pl.loop(0, half // blk)
        def _(i):
            snd[h, pl.ds(pl.multiple_of(off + i * blk, 16), blk), :] = acc[
                pl.ds(pl.multiple_of(base + i * blk, 16), blk), pl.ds(h * LANES, LANES)].astype(BF)

        rs_copy(part, h, s).start()

    def rs_recv(part, h, s):
        acc, snd, rcv, ss, rs, order = part
        off, half = size - (size >> s), size >> (s + 1)
        base = rs_base(order, s + 1)
        blk = min(128, half)
        rs_copy(part, h, s).wait_recv()

        @pl.loop(0, half // blk)
        def _(i):
            at = pl.ds(pl.multiple_of(base + i * blk, 16), blk)
            acc[at, pl.ds(h * LANES, LANES)] += rcv[h, pl.ds(pl.multiple_of(off + i * blk, 16), blk), :].astype(F32)

    def rs_next(h, s):
        for part in (down, upw):
            rs_recv(part, h, s)
            if s + 1 < logn:
                rs_send(part, h, s + 1)

    down = (acc_d, snd_d, rcv_d, d_send, d_recv, order_d)
    upw = (acc_u, snd_u, rcv_u, u_send, u_recv, order_u)
    halves = TILE // LANES
    for h in range(halves):
        rs_send(down, h, 0)
        rs_send(upw, h, 0)

    gnorm = gn[...]
    normed = norm_s[...]
    gain_row = jnp.sum(gnorm * normed, axis=0, keepdims=True)
    bias_row = jnp.sum(gnorm, axis=0, keepdims=True)
    scaled = gnorm * gain_ref[...]
    grad_conv = (
        scaled
        - jnp.mean(scaled, axis=1, keepdims=True)
        - normed * jnp.mean(scaled * normed, axis=1, keepdims=True)
    ) * inv_s[...]
    gc[...] = grad_conv
    prepare(ext_g, pk_g, top_g, grad_conv.astype(BF))
    send_all(ext_g, pk_g, top_g, 1)
    taps = dk_ref.shape[0]
    for ct in range(chans // 128):
        sm[ct, pl.ds(48, 8), :] = jnp.zeros((8, 128), F32)
        sm[ct, pl.ds(taps, 1), :] = gain_row[:, ct * 128:(ct + 1) * 128]
        sm[ct, pl.ds(taps + 1, 1), :] = bias_row[:, ct * 128:(ct + 1) * 128]

    out_ref[...] = (state_ref[...].astype(F32) + mask * br[...]).astype(BF)

    for h in range(halves):
        rs_next(h, 0)

    @pl.loop(0, chans // 128)
    def _(ct):
        ls = lanes(ct)
        g = gc[:, ls].reshape(lat, cols, 128)
        for b in range(7):
            window = sh[b, :, :, ls]
            for a in range(7):
                part = jnp.sum(g * window[a:a + lat], axis=0)
                sm[ct, pl.ds(7 * a + b, 1), :] = jnp.sum(part, axis=0, keepdims=True)

    quarters = chans // 512
    b0, b1 = bit_of(0), bit_of(1)
    keep0, send0 = pl.ds(2 * quarters * b0, 2 * quarters), pl.ds(2 * quarters * (1 - b0), 2 * quarters)
    keep1 = pl.ds(quarters * (2 * b0 + b1), quarters)
    send1 = pl.ds(quarters * (2 * b0 + 1 - b1), quarters)

    def sm_copy(s):
        if s == 0:
            src, dst, bit = sm.at[send0], sm_r.at[pl.ds(0, 2 * quarters)], 0
        elif s == 1:
            src, dst, bit = sm.at[send1], sm_r.at[pl.ds(2 * quarters, quarters)], 1
        elif s < logn:
            src, dst, bit = cur.at[s], cur_r.at[s], s
        elif s == logn:
            src, dst, bit = sums_s.at[keep1], sums_s.at[keep1], 1
        else:
            src, dst, bit = sums_s.at[keep0], sums_s.at[keep0], 0
        return remote(src, dst, s_send.at[s], s_recv.at[s], partner(bit))

    def sm_step(s):
        sm_copy(s).wait_recv()
        if s == 0:
            sm[keep0] = sm[keep0] + sm_r[pl.ds(0, 2 * quarters)]
        elif s == 1:
            cur[2] = sm[keep1] + sm_r[pl.ds(2 * quarters, quarters)]
        elif s < logn - 1:
            cur[s + 1] = cur[s] + cur_r[s]
        elif s == logn - 1:
            sums_s[keep1] = cur[s] + cur_r[s]
        if s < logn + 1:
            sm_copy(s + 1).start()

    sm_copy(0).start()

    wait_halo(ext_g, pk_g, 1)
    put_shifts(ext_g, sh_g)
    sh_g[:, pl.ds(lat + 3, 3)] = jnp.zeros((7, 3, cols, chans), F32)
    sm_step(0)
    pass_top(top_g, 1)
    sm_step(1)
    wait_top(top_g, 1)

    def store_facing(k, b, ls, val):
        sh_f[b, k, :, ls] = val

    put_fold(top_g, sel, store_facing)

    @pl.loop(0, chans // 128)
    def _(ct):
        ls = lanes(ct)
        acc = jnp.zeros((lat, cols, 128), F32)
        fold = [jnp.zeros((cols, 128), F32) for _ in range(3)]
        for b in range(7):
            window = sh_g[b, :, :, ls]
            for a in range(7):
                tap = dk_ref[pl.ds(48 - (7 * a + b), 1), ls].reshape(1, 1, 128)
                acc = acc + tap * window[a:a + lat]
            for r in range(3):
                for j in range(3):
                    a = 8 - r - j
                    if a <= 6:
                        tap = dk_ref[pl.ds(7 * a + b, 1), ls]
                        fold[r] = fold[r] + tap * sh_f[b, j, :, ls]
        acc = acc.reshape(cells, 128)
        gc[:, ls] = acc
        for r in range(3):
            gc[pl.ds((lat - 3 + r) * cols, cols), ls] += fold[r]

    gstate_ref[...] = (cot_ref[...].astype(F32) + mask * gc[...]).astype(BF)

    steps = list(range(2, logn + 2))
    for s in range(1, logn):
        for h in range(halves):
            rs_next(h, s)
            if steps:
                sm_step(steps.pop(0))
    for s in steps:
        sm_step(s)

    base_d = pl.multiple_of(rs_base(order_d, logn), 8)
    base_u = rs_base(order_u, logn)
    gdn_ref[...] = acc_d[pl.ds(base_d, rows_d), :] * scale
    for t in range(hid // TILE):
        gup_ref[:, pl.ds(t * TILE, TILE)] = acc_u[pl.ds(pl.multiple_of(base_u + t * rows_u, 8), rows_u), :] * scale
    for ct in range(chans // 128):
        ls = pl.ds(ct * 128, 128)
        gk_ref[:, ls] = sums_s[ct, pl.ds(0, taps), :] * scale
        ggain_ref[:, ls] = sums_s[ct, pl.ds(taps, 1), :] * scale
        gbias_ref[:, ls] = sums_s[ct, pl.ds(taps + 1, 1), :] * scale

    for e_ref, p_ref, t_ref, w in ((ext, pk, top, 0), (ext_g, pk_g, top_g, 1)):
        for c in halo_copies(e_ref, p_ref, w):
            c.wait_send()

        @pl.loop(1, pairs)
        def _(k):
            top_copy(t_ref, w, k).wait_send()

        pair_copy(t_ref, w).wait_send()

    for s in range(logn):
        for h in range(halves):
            rs_copy(down, h, s).wait_send()
            rs_copy(upw, h, s).wait_send()
    for s in range(logn + 2):
        sm_copy(s).wait_send()


def finish(*refs):
    count = len(refs) // 2
    for src, dst in zip(refs[:count], refs[count:]):
        dst[...] = src[...]


def on_device(
    state_in, ocean_mask, fold_partner, depth_kernel, norm_gain, norm_bias, w_up, w_down, cotangent
):
    lat, cols, chans = state_in.shape
    hid = w_up.shape[1]
    n = lax.axis_size("lon")
    logn = n.bit_length() - 1
    cells = lat * cols
    shifts, packs = shift_matrices(lat, cols)
    depth = shifts.shape[1]
    rows = hid * chans // TILE
    vm = pl.BlockSpec(memory_space=pltpu.VMEM)
    hbm = pl.BlockSpec(memory_space=pl.ANY)
    sem = pltpu.SemaphoreType.DMA
    outs = pl.pallas_call(
        functools.partial(kernel, n, lat, cols),
        out_shape=(
            jax.ShapeDtypeStruct((cells, chans), BF),
            jax.ShapeDtypeStruct((cells, chans), BF),
            jax.ShapeDtypeStruct((chans // n, hid), F32),
            jax.ShapeDtypeStruct((hid // n, chans), F32),
            jax.ShapeDtypeStruct(depth_kernel.shape, F32),
            jax.ShapeDtypeStruct((1, chans), F32),
            jax.ShapeDtypeStruct((1, chans), F32),
        ),
        in_specs=[pl.BlockSpec(memory_space=pltpu.SMEM)] + [hbm] * 10,
        out_specs=(vm,) * 7,
        scratch_shapes=[
            pltpu.VMEM((cells, chans), BF),
            pltpu.VMEM((cells, 1), F32),
            pltpu.VMEM(packs.shape, BF),
            pltpu.VMEM(shifts.shape, BF),
            pltpu.VMEM(depth_kernel.shape, F32),
            pltpu.VMEM((1, chans), F32),
            pltpu.VMEM((1, chans), F32),
            pltpu.VMEM((cells, chans), BF),
            pltpu.VMEM((chans, hid), BF),
            pltpu.VMEM((hid, chans), BF),
            pltpu.VMEM((depth, chans), BF),
            pltpu.VMEM((depth, chans), BF),
            pltpu.VMEM((6 * lat, chans), BF),
            pltpu.VMEM((6 * lat, chans), BF),
            pltpu.VMEM((2, n // 2, 6 * cols, chans // 2), BF),
            pltpu.VMEM((2, n // 2, 6 * cols, chans // 2), BF),
            pltpu.VMEM((7, lat + 6, cols, chans), F32),
            pltpu.VMEM((7, lat + 6, cols, chans), F32),
            pltpu.VMEM((7, 3, cols, chans), F32),
            pltpu.VMEM((cells, chans), F32),
            pltpu.VMEM((cells, chans), BF),
            pltpu.VMEM((cells, 1), F32),
            pltpu.VMEM((cells, chans), BF),
            pltpu.VMEM((cells, chans), F32),
            pltpu.VMEM((cells, chans), F32),
            pltpu.VMEM((cells, chans), F32),
            pltpu.VMEM((rows, TILE), F32),
            pltpu.VMEM((rows, TILE), F32),
            pltpu.VMEM((TILE // LANES, rows, LANES), BF),
            pltpu.VMEM((TILE // LANES, rows, LANES), BF),
            pltpu.VMEM((TILE // LANES, rows, LANES), BF),
            pltpu.VMEM((TILE // LANES, rows, LANES), BF),
            pltpu.VMEM((chans // 128, 56, 128), F32),
            pltpu.VMEM((3 * chans // 512, 56, 128), F32),
            pltpu.VMEM((logn, chans // 512, 56, 128), F32),
            pltpu.VMEM((logn, chans // 512, 56, 128), F32),
            pltpu.VMEM((chans // 128, 56, 128), F32),
            sem((10,)),
            sem((4,)),
            sem((4,)),
            sem((n + 2,)),
            sem((n + 2,)),
            sem((TILE // LANES * logn,)),
            sem((TILE // LANES * logn,)),
            sem((TILE // LANES * logn,)),
            sem((TILE // LANES * logn,)),
            sem((logn + 2,)),
            sem((logn + 2,)),
        ],
        compiler_params=pltpu.CompilerParams(
            collective_id=0, has_side_effects=True, vmem_limit_bytes=64 * 1024 * 1024
        ),
    )(
        fold_partner,
        state_in.reshape(cells, chans),
        ocean_mask.astype(F32).reshape(cells, 1),
        jnp.asarray(packs, BF),
        jnp.asarray(shifts, BF),
        depth_kernel,
        norm_gain.reshape(1, chans),
        norm_bias.reshape(1, chans),
        cotangent.reshape(cells, chans),
        w_up,
        w_down,
    )
    out, gstate, gup, gdn, gk, ggain, gbias = pl.pallas_call(
        finish,
        out_shape=tuple(jax.ShapeDtypeStruct(o.shape, o.dtype) for o in outs),
        in_specs=[vm] * 7,
        out_specs=(vm,) * 7,
    )(*outs)
    return (
        out.reshape(lat, cols, chans),
        gstate.reshape(lat, cols, chans),
        gup,
        gdn,
        gk,
        ggain.reshape(chans),
        gbias.reshape(chans),
    )


def solution(mesh):
    return jax.shard_map(
        on_device,
        mesh=mesh,
        in_specs=(
            P("ens", "lon", None),
            P(None, "lon"),
            P(),
            P(),
            P(),
            P(),
            P(),
            P(),
            P("ens", "lon", None),
        ),
        out_specs=(
            P("ens", "lon", None),
            P("ens", "lon", None),
            P(("ens", "lon"), None),
            P(("ens", "lon"), None),
            P("ens", None),
            P("ens"),
            P("ens"),
        ),
        check_vma=False,
    )
```

```python
import functools
import math

import jax
import jax.numpy as jnp
import numpy as np
from jax import lax
from jax.experimental import pallas as pl
from jax.experimental.pallas import tpu as pltpu
from jax.sharding import PartitionSpec as P

EPS = 1e-06
TILE = 512
LANES = 256
BF = jnp.bfloat16
F32 = jnp.float32
GELU_A = math.sqrt(2.0 / math.pi)
GELU_B = 0.044715


def shift_matrices(lat, cols):
    own0, right0 = 3 * lat, 3 * lat + lat * cols
    depth = -(-(right0 + 3 * lat) // 128) * 128
    shifts = np.zeros((7, lat, cols, depth), np.float32)
    for b in range(7):
        for i in range(cols):
            e = b + i
            for r in range(lat):
                if e < 3:
                    src = r * 3 + e
                elif e < cols + 3:
                    src = own0 + r * cols + e - 3
                else:
                    src = right0 + r * 3 + e - cols - 3
                shifts[b, r, i, src] = 1.0
    packs = np.zeros((2, lat, 3, lat * cols), np.float32)
    for r in range(lat):
        for k in range(3):
            packs[0, r, k, r * cols + k] = 1.0
            packs[1, r, k, r * cols + cols - 3 + k] = 1.0
    return shifts.reshape(7 * lat * cols, depth), packs.reshape(6 * lat, lat * cols)


def place(chunk, order):
    pos = 0
    for bit in order:
        pos = pos * 2 + (chunk // 2**bit) % 2
    return pos


def dot(a, b, dims=((1,), (0,))):
    return lax.dot_general(a, b, (dims, ((), ())), preferred_element_type=F32)


def kernel(
    n, lat, cols,
    fold_ref, state_hbm, mask_hbm, pack_hbm, shift_hbm, dk_hbm, gain_hbm, bias_hbm, cot_hbm, wup_hbm, wdn_hbm,
    out_ref, gstate_ref, gup_ref, gdn_ref, gk_ref, ggain_ref, gbias_ref,
    state_ref, mask_ref, pack_ref, shift_ref, dk_ref, gain_ref, bias_ref, cot_ref, wup, wdn, ext, ext_g, pk, pk_g, top, top_g, sh, sh_g, sh_f, norm_s, nout_s, inv_s, ups, br, gn, gc,
    acc_d, acc_u, snd_d, snd_u, rcv_d, rcv_u, sm, sm_r, cur, cur_r, sums_s,
    w_sem, h_send, h_recv, t_send, t_recv, d_send, d_recv, u_send, u_recv, s_send, s_recv,
):
    chans = state_ref.shape[1]
    hid = wup.shape[1]
    cells = lat * cols
    total = n * cols
    logn = n.bit_length() - 1
    scale = 1.0 / math.sqrt(lat * total)
    me = lax.axis_index("lon")
    order_d = list(range(logn))
    order_u = [0, 2, 1] + list(range(3, logn))
    right, left = (me + 1) % n, (me + n - 1) % n
    half_c = chans // 2

    loads = [
        pltpu.make_async_copy(src, dst, w_sem.at[i])
        for i, (src, dst) in enumerate((
            (state_hbm, state_ref), (mask_hbm, mask_ref), (pack_hbm, pack_ref), (shift_hbm, shift_ref),
            (dk_hbm, dk_ref), (gain_hbm, gain_ref), (bias_hbm, bias_ref), (cot_hbm, cot_ref),
            (wup_hbm, wup), (wdn_hbm, wdn)))
    ]
    for c in loads:
        c.start()

    barrier = pltpu.get_barrier_semaphore()

    @pl.loop(1, n)
    def _(k):
        pl.semaphore_signal(barrier, inc=1, device_id={"lon": (me + k) % n}, device_id_type=pl.DeviceIdType.MESH)

    for c in loads[:3]:
        c.wait()
    mask = mask_ref[...]
    mask_bf = mask.astype(BF)

    def remote(src, dst, ss, rs, dev):
        return pltpu.make_async_remote_copy(
            src_ref=src, dst_ref=dst, send_sem=ss, recv_sem=rs,
            device_id={"lon": dev}, device_id_type=pl.DeviceIdType.MESH,
        )

    own0, right0, edge = 3 * lat, 3 * lat + cells, 3 * lat

    def halo_copies(e_ref, p_ref, w):
        return [
            remote(p_ref.at[pl.ds(edge, edge)], e_ref.at[pl.ds(0, edge)], h_send.at[2 * w], h_recv.at[2 * w], right),
            remote(p_ref.at[pl.ds(0, edge)], e_ref.at[pl.ds(right0, edge)], h_send.at[2 * w + 1], h_recv.at[2 * w + 1], left),
        ]

    mine, pairs = me % 2, n // 2

    def top_copy(t_ref, w, k):
        block = t_ref.at[mine, me // 2]
        at = w * (pairs + 1) + k
        return remote(block, block, t_send.at[at], t_recv.at[at], (me + 2 * k) % n)

    def pair_copy(t_ref, w):
        at = w * (pairs + 1) + pairs
        return remote(t_ref.at[mine], t_ref.at[mine], t_send.at[at], t_recv.at[at], me + 1 - 2 * mine)

    def prepare(e_ref, p_ref, t_ref, values_bf):
        e_ref[pl.ds(own0, cells), :] = values_bf
        e_ref[pl.ds(right0 + edge, e_ref.shape[0] - right0 - edge), :] = jnp.zeros(
            (e_ref.shape[0] - right0 - edge, chans), BF)
        p_ref[...] = dot(pack_ref[...], values_bf).astype(BF)
        for k in range(3):
            row = values_bf[(lat - 3 + k) * cols:(lat - 2 + k) * cols].astype(F32)
            t_ref[mine, me // 2, pl.ds(k * 2 * cols, 2 * cols), :] = jnp.concatenate(
                [row[:, :half_c], row[:, half_c:]], axis=0).astype(BF)

    def send_all(e_ref, p_ref, t_ref, w):
        for c in halo_copies(e_ref, p_ref, w):
            c.start()

        @pl.loop(1, pairs)
        def _(k):
            top_copy(t_ref, w, k).start()

    def wait_halo(e_ref, p_ref, w):
        for c in halo_copies(e_ref, p_ref, w):
            c.wait_recv()

    def pass_top(t_ref, w):
        @pl.loop(1, pairs)
        def _(k):
            top_copy(t_ref, w, k).wait_recv()

        pair_copy(t_ref, w).start()

    def wait_top(t_ref, w):
        pair_copy(t_ref, w).wait_recv()

    def put_shifts(e_ref, s_ref):
        s_ref[:, pl.ds(0, 3)] = jnp.zeros((7, 3, cols, chans), F32)
        for b in range(7):
            part = dot(shift_ref[pl.ds(b * cells, cells), :], e_ref[...])
            s_ref[b, pl.ds(3, lat)] = part.reshape(lat, cols, chans)

    def put_fold(t_ref, sel, store):
        for k in range(3):
            rows = t_ref[:, :, pl.ds(k * 2 * cols, 2 * cols), :].reshape(n * 2 * cols, half_c)
            got = dot(sel, rows).reshape(2, 7, cols, half_c)
            for h in range(2):
                for b in range(7):
                    store(k, b, pl.ds(h * half_c, half_c), got[h, b])

    def lanes(ct):
        return pl.ds(pl.multiple_of(ct * 128, 128), 128)

    state = state_ref[...]
    prepare(ext, pk, top, state * mask_bf)
    pl.semaphore_wait(barrier, n - 1)
    send_all(ext, pk, top, 0)

    m_id = lax.broadcasted_iota(jnp.int32, (14 * cols, n * 2 * cols), 0)
    q_id = lax.broadcasted_iota(jnp.int32, (14 * cols, n * 2 * cols), 1)
    half_m = jnp.where(m_id >= 7 * cols, 1, 0)
    m_in = m_id - half_m * (7 * cols)
    want = fold_ref[0] - me * cols + 3 - (m_in // cols + m_in % cols)
    want = jnp.where(want < 0, want + total, want)
    want = jnp.where(want < 0, want + total, want)
    want = jnp.where(want >= total, want - total, want)
    slot = q_id // (2 * cols)
    have = (2 * (slot % pairs) + slot // pairs) * cols + q_id % cols
    half_q = (q_id // cols) % 2
    sel = jnp.where((have == want) & (half_q == half_m), 1.0, 0.0).astype(BF)

    for c in loads[3:8]:
        c.wait()
    cot = cot_ref[...]
    upstream = cot * mask_bf
    ups[...] = upstream

    wait_halo(ext, pk, 0)
    put_shifts(ext, sh)
    pass_top(top, 0)
    wait_top(top, 0)

    def store_north(k, b, ls, val):
        sh[b, lat + 5 - k, :, ls] = val

    put_fold(top, sel, store_north)

    @pl.loop(0, chans // 128)
    def _(ct):
        ls = lanes(ct)
        acc = jnp.zeros((lat, cols, 128), F32)
        for b in range(7):
            window = sh[b, :, :, ls]
            for a in range(7):
                tap = dk_ref[pl.ds(7 * a + b, 1), ls].reshape(1, 1, 128)
                acc = acc + tap * window[a:a + lat]
        norm_s[:, ls] = acc.reshape(cells, 128)

    conv = norm_s[...]
    centred = conv - jnp.mean(conv, axis=1, keepdims=True)
    inv = 1.0 / jnp.sqrt(jnp.mean(centred * centred, axis=1, keepdims=True) + EPS)
    inv_s[...] = inv
    normed = centred * inv
    norm_s[...] = normed
    nout_s[...] = (normed * gain_ref[...] + bias_ref[...]).astype(BF)
    for c in loads[8:]:
        c.wait()
    br[...] = jnp.zeros_like(br)
    gn[...] = jnp.zeros_like(gn)
    rows_d, rows_u = hid // n, chans // n
    per_tile = TILE // rows_d

    @pl.loop(0, hid // TILE)
    def _(t):
        hs = pl.ds(pl.multiple_of(t * TILE, TILE), TILE)
        nout = nout_s[...]
        up = ups[...]
        w1 = wup[:, hs]
        w2 = wdn[hs, :]
        v = dot(nout, w1)
        v2 = v * v
        th = jnp.tanh(GELU_A * (v + GELU_B * (v2 * v)))
        u = (0.5 * v * (1.0 + th)).astype(BF)
        br[...] += dot(u, w2)
        gd = dot(u, up, ((0,), (0,)))
        for cc in range(per_tile):
            pos = place(t * per_tile + cc, order_d)
            acc_d[pl.ds(pl.multiple_of(pos * rows_d, 8), rows_d), :] = gd[cc * rows_d:(cc + 1) * rows_d]
        gh = dot(up, w2, ((1,), (1,)))
        slope = 0.5 * (1.0 + th) + (0.5 * GELU_A) * v * (1.0 - th * th) * (1.0 + (3.0 * GELU_B) * v2)
        gp = (gh * slope).astype(BF)
        gn[...] += dot(gp, w1, ((1,), (1,)))
        gu = dot(nout, gp, ((0,), (0,)))
        for c in range(n):
            base = place(c, order_u) * (hid * chans // n // TILE)
            acc_u[pl.ds(pl.multiple_of(base + t * rows_u, 8), rows_u), :] = gu[c * rows_u:(c + 1) * rows_u]

    def bit_of(bit):
        return (me // 2**bit) % 2

    def partner(bit):
        return me + (1 - 2 * bit_of(bit)) * 2**bit

    size = acc_d.shape[0]

    def rs_base(order, s):
        base = 0
        for k in range(s):
            base = base + bit_of(order[k]) * (size >> (k + 1))
        return base

    def rs_copy(part, h, s):
        acc, snd, rcv, ss, rs, order = part
        at = pl.ds(size - (size >> s), size >> (s + 1))
        sem = h * logn + s
        return remote(snd.at[h, at], rcv.at[h, at], ss.at[sem], rs.at[sem], partner(order[s]))

    def rs_send(part, h, s):
        acc, snd, rcv, ss, rs, order = part
        off, half = size - (size >> s), size >> (s + 1)
        base = rs_base(order, s) + (1 - bit_of(order[s])) * half
        blk = min(128, half)

        @pl.loop(0, half // blk)
        def _(i):
            snd[h, pl.ds(pl.multiple_of(off + i * blk, 16), blk), :] = acc[
                pl.ds(pl.multiple_of(base + i * blk, 16), blk), pl.ds(h * LANES, LANES)].astype(BF)

        rs_copy(part, h, s).start()

    def rs_recv(part, h, s):
        acc, snd, rcv, ss, rs, order = part
        off, half = size - (size >> s), size >> (s + 1)
        base = rs_base(order, s + 1)
        blk = min(128, half)
        rs_copy(part, h, s).wait_recv()

        @pl.loop(0, half // blk)
        def _(i):
            at = pl.ds(pl.multiple_of(base + i * blk, 16), blk)
            acc[at, pl.ds(h * LANES, LANES)] += rcv[h, pl.ds(pl.multiple_of(off + i * blk, 16), blk), :].astype(F32)

    def rs_next(h, s):
        for part in (down, upw):
            rs_recv(part, h, s)
            if s + 1 < logn:
                rs_send(part, h, s + 1)

    down = (acc_d, snd_d, rcv_d, d_send, d_recv, order_d)
    upw = (acc_u, snd_u, rcv_u, u_send, u_recv, order_u)
    halves = TILE // LANES
    for h in range(halves):
        rs_send(down, h, 0)
        rs_send(upw, h, 0)

    gnorm = gn[...]
    normed = norm_s[...]
    gain_row = jnp.sum(gnorm * normed, axis=0, keepdims=True)
    bias_row = jnp.sum(gnorm, axis=0, keepdims=True)
    scaled = gnorm * gain_ref[...]
    grad_conv = (
        scaled
        - jnp.mean(scaled, axis=1, keepdims=True)
        - normed * jnp.mean(scaled * normed, axis=1, keepdims=True)
    ) * inv_s[...]
    gc[...] = grad_conv
    prepare(ext_g, pk_g, top_g, grad_conv.astype(BF))
    send_all(ext_g, pk_g, top_g, 1)
    taps = dk_ref.shape[0]
    for ct in range(chans // 128):
        sm[ct, pl.ds(48, 8), :] = jnp.zeros((8, 128), F32)
        sm[ct, pl.ds(taps, 1), :] = gain_row[:, ct * 128:(ct + 1) * 128]
        sm[ct, pl.ds(taps + 1, 1), :] = bias_row[:, ct * 128:(ct + 1) * 128]

    for h in range(halves):
        rs_next(h, 0)

    out_ref[...] = (state_ref[...].astype(F32) + mask * br[...]).astype(BF)

    @pl.loop(0, chans // 128)
    def _(ct):
        ls = lanes(ct)
        g = gc[:, ls].reshape(lat, cols, 128)
        for b in range(7):
            window = sh[b, :, :, ls]
            for a in range(7):
                part = jnp.sum(g * window[a:a + lat], axis=0)
                sm[ct, pl.ds(7 * a + b, 1), :] = jnp.sum(part, axis=0, keepdims=True)

    quarters = chans // 512
    b0, b1 = bit_of(0), bit_of(1)
    keep0, send0 = pl.ds(2 * quarters * b0, 2 * quarters), pl.ds(2 * quarters * (1 - b0), 2 * quarters)
    keep1 = pl.ds(quarters * (2 * b0 + b1), quarters)
    send1 = pl.ds(quarters * (2 * b0 + 1 - b1), quarters)

    def sm_copy(s):
        if s == 0:
            src, dst, bit = sm.at[send0], sm_r.at[pl.ds(0, 2 * quarters)], 0
        elif s == 1:
            src, dst, bit = sm.at[send1], sm_r.at[pl.ds(2 * quarters, quarters)], 1
        elif s < logn:
            src, dst, bit = cur.at[s], cur_r.at[s], s
        elif s == logn:
            src, dst, bit = sums_s.at[keep1], sums_s.at[keep1], 1
        else:
            src, dst, bit = sums_s.at[keep0], sums_s.at[keep0], 0
        return remote(src, dst, s_send.at[s], s_recv.at[s], partner(bit))

    def sm_step(s):
        sm_copy(s).wait_recv()
        if s == 0:
            sm[keep0] = sm[keep0] + sm_r[pl.ds(0, 2 * quarters)]
        elif s == 1:
            cur[2] = sm[keep1] + sm_r[pl.ds(2 * quarters, quarters)]
        elif s < logn - 1:
            cur[s + 1] = cur[s] + cur_r[s]
        elif s == logn - 1:
            sums_s[keep1] = cur[s] + cur_r[s]
        if s < logn + 1:
            sm_copy(s + 1).start()

    sm_copy(0).start()

    wait_halo(ext_g, pk_g, 1)
    put_shifts(ext_g, sh_g)
    sh_g[:, pl.ds(lat + 3, 3)] = jnp.zeros((7, 3, cols, chans), F32)
    sm_step(0)
    pass_top(top_g, 1)
    sm_step(1)
    wait_top(top_g, 1)

    def store_facing(k, b, ls, val):
        sh_f[b, k, :, ls] = val

    put_fold(top_g, sel, store_facing)

    @pl.loop(0, chans // 128)
    def _(ct):
        ls = lanes(ct)
        acc = jnp.zeros((lat, cols, 128), F32)
        fold = [jnp.zeros((cols, 128), F32) for _ in range(3)]
        for b in range(7):
            window = sh_g[b, :, :, ls]
            for a in range(7):
                tap = dk_ref[pl.ds(48 - (7 * a + b), 1), ls].reshape(1, 1, 128)
                acc = acc + tap * window[a:a + lat]
            for r in range(3):
                for j in range(3):
                    a = 8 - r - j
                    if a <= 6:
                        tap = dk_ref[pl.ds(7 * a + b, 1), ls]
                        fold[r] = fold[r] + tap * sh_f[b, j, :, ls]
        acc = acc.reshape(cells, 128)
        gc[:, ls] = acc
        for r in range(3):
            gc[pl.ds((lat - 3 + r) * cols, cols), ls] += fold[r]

    gstate_ref[...] = (cot_ref[...].astype(F32) + mask * gc[...]).astype(BF)

    steps = list(range(2, logn + 2))
    for s in range(1, logn):
        for h in range(halves):
            rs_next(h, s)
            if steps:
                sm_step(steps.pop(0))
    for s in steps:
        sm_step(s)

    base_d = pl.multiple_of(rs_base(order_d, logn), 8)
    base_u = rs_base(order_u, logn)
    gdn_ref[...] = acc_d[pl.ds(base_d, rows_d), :] * scale
    for t in range(hid // TILE):
        gup_ref[:, pl.ds(t * TILE, TILE)] = acc_u[pl.ds(pl.multiple_of(base_u + t * rows_u, 8), rows_u), :] * scale
    for ct in range(chans // 128):
        ls = pl.ds(ct * 128, 128)
        gk_ref[:, ls] = sums_s[ct, pl.ds(0, taps), :] * scale
        ggain_ref[:, ls] = sums_s[ct, pl.ds(taps, 1), :] * scale
        gbias_ref[:, ls] = sums_s[ct, pl.ds(taps + 1, 1), :] * scale

    for e_ref, p_ref, t_ref, w in ((ext, pk, top, 0), (ext_g, pk_g, top_g, 1)):
        for c in halo_copies(e_ref, p_ref, w):
            c.wait_send()

        @pl.loop(1, pairs)
        def _(k):
            top_copy(t_ref, w, k).wait_send()

        pair_copy(t_ref, w).wait_send()

    for s in range(logn):
        for h in range(halves):
            rs_copy(down, h, s).wait_send()
            rs_copy(upw, h, s).wait_send()
    for s in range(logn + 2):
        sm_copy(s).wait_send()


def finish(*refs):
    count = len(refs) // 2
    for src, dst in zip(refs[:count], refs[count:]):
        dst[...] = src[...]


def on_device(
    state_in, ocean_mask, fold_partner, depth_kernel, norm_gain, norm_bias, w_up, w_down, cotangent
):
    lat, cols, chans = state_in.shape
    hid = w_up.shape[1]
    n = lax.axis_size("lon")
    logn = n.bit_length() - 1
    cells = lat * cols
    shifts, packs = shift_matrices(lat, cols)
    depth = shifts.shape[1]
    rows = hid * chans // TILE
    vm = pl.BlockSpec(memory_space=pltpu.VMEM)
    hbm = pl.BlockSpec(memory_space=pl.ANY)
    sem = pltpu.SemaphoreType.DMA
    outs = pl.pallas_call(
        functools.partial(kernel, n, lat, cols),
        out_shape=(
            jax.ShapeDtypeStruct((cells, chans), BF),
            jax.ShapeDtypeStruct((cells, chans), BF),
            jax.ShapeDtypeStruct((chans // n, hid), F32),
            jax.ShapeDtypeStruct((hid // n, chans), F32),
            jax.ShapeDtypeStruct(depth_kernel.shape, F32),
            jax.ShapeDtypeStruct((1, chans), F32),
            jax.ShapeDtypeStruct((1, chans), F32),
        ),
        in_specs=[pl.BlockSpec(memory_space=pltpu.SMEM)] + [hbm] * 10,
        out_specs=(vm,) * 7,
        scratch_shapes=[
            pltpu.VMEM((cells, chans), BF),
            pltpu.VMEM((cells, 1), F32),
            pltpu.VMEM(packs.shape, BF),
            pltpu.VMEM(shifts.shape, BF),
            pltpu.VMEM(depth_kernel.shape, F32),
            pltpu.VMEM((1, chans), F32),
            pltpu.VMEM((1, chans), F32),
            pltpu.VMEM((cells, chans), BF),
            pltpu.VMEM((chans, hid), BF),
            pltpu.VMEM((hid, chans), BF),
            pltpu.VMEM((depth, chans), BF),
            pltpu.VMEM((depth, chans), BF),
            pltpu.VMEM((6 * lat, chans), BF),
            pltpu.VMEM((6 * lat, chans), BF),
            pltpu.VMEM((2, n // 2, 6 * cols, chans // 2), BF),
            pltpu.VMEM((2, n // 2, 6 * cols, chans // 2), BF),
            pltpu.VMEM((7, lat + 6, cols, chans), F32),
            pltpu.VMEM((7, lat + 6, cols, chans), F32),
            pltpu.VMEM((7, 3, cols, chans), F32),
            pltpu.VMEM((cells, chans), F32),
            pltpu.VMEM((cells, chans), BF),
            pltpu.VMEM((cells, 1), F32),
            pltpu.VMEM((cells, chans), BF),
            pltpu.VMEM((cells, chans), F32),
            pltpu.VMEM((cells, chans), F32),
            pltpu.VMEM((cells, chans), F32),
            pltpu.VMEM((rows, TILE), F32),
            pltpu.VMEM((rows, TILE), F32),
            pltpu.VMEM((TILE // LANES, rows, LANES), BF),
            pltpu.VMEM((TILE // LANES, rows, LANES), BF),
            pltpu.VMEM((TILE // LANES, rows, LANES), BF),
            pltpu.VMEM((TILE // LANES, rows, LANES), BF),
            pltpu.VMEM((chans // 128, 56, 128), F32),
            pltpu.VMEM((3 * chans // 512, 56, 128), F32),
            pltpu.VMEM((logn, chans // 512, 56, 128), F32),
            pltpu.VMEM((logn, chans // 512, 56, 128), F32),
            pltpu.VMEM((chans // 128, 56, 128), F32),
            sem((10,)),
            sem((4,)),
            sem((4,)),
            sem((n + 2,)),
            sem((n + 2,)),
            sem((TILE // LANES * logn,)),
            sem((TILE // LANES * logn,)),
            sem((TILE // LANES * logn,)),
            sem((TILE // LANES * logn,)),
            sem((logn + 2,)),
            sem((logn + 2,)),
        ],
        compiler_params=pltpu.CompilerParams(
            collective_id=0, has_side_effects=True, vmem_limit_bytes=64 * 1024 * 1024
        ),
    )(
        fold_partner,
        state_in.reshape(cells, chans),
        ocean_mask.astype(F32).reshape(cells, 1),
        jnp.asarray(packs, BF),
        jnp.asarray(shifts, BF),
        depth_kernel,
        norm_gain.reshape(1, chans),
        norm_bias.reshape(1, chans),
        cotangent.reshape(cells, chans),
        w_up,
        w_down,
    )
    out, gstate, gup, gdn, gk, ggain, gbias = pl.pallas_call(
        finish,
        out_shape=tuple(jax.ShapeDtypeStruct(o.shape, o.dtype) for o in outs),
        in_specs=[vm] * 7,
        out_specs=(vm,) * 7,
    )(*outs)
    return (
        out.reshape(lat, cols, chans),
        gstate.reshape(lat, cols, chans),
        gup,
        gdn,
        gk,
        ggain.reshape(chans),
        gbias.reshape(chans),
    )


def solution(mesh):
    return jax.shard_map(
        on_device,
        mesh=mesh,
        in_specs=(
            P("ens", "lon", None),
            P(None, "lon"),
            P(),
            P(),
            P(),
            P(),
            P(),
            P(),
            P("ens", "lon", None),
        ),
        out_specs=(
            P("ens", "lon", None),
            P("ens", "lon", None),
            P(("ens", "lon"), None),
            P(("ens", "lon"), None),
            P("ens", None),
            P("ens"),
            P("ens"),
        ),
        check_vma=False,
    )
```
